32 devices in a mesh: ctx: 8 (over z, x), exp: 4 (over y, core).
Axes of the slice: x: 2, y: 2, z: 4, core: 2. Of those that a mesh axis runs over, the one named last changes fastest.
Arguments:
- queries: bfloat16 [2048, 36864], P('ctx', 'exp'), may hold values from -8 to 8
- latent: bfloat16 [2048, 576], P('ctx'), may hold values from -8 to 8
- block_order: int32 [16], replicated, may hold values from 0 to 15, each once
- w_uv: bfloat16 [64, 512, 128], P('exp'), may hold values from -0.25 to 0.25
- w_o: bfloat16 [8192, 7168], P('exp', 'ctx'), may hold values from -0.0625 to 0.0625
- residual: bfloat16 [2048, 7168], P(('ctx', 'exp')), may hold values from -4 to 4
- norm_gain: bfloat16 [7168], replicated, may hold values from 0.099609375 to 1.8984375
- routes: int32 [2048, 8], P(('ctx', 'exp')), may hold values from 0 to 255, as said below
- route_scores: float32 [2048, 8], P(('ctx', 'exp')), may hold values from 0.05 to 1
- w_gate: bfloat16 [4, 7168, 2048], P('exp', None, 'ctx'), may hold values from -0.0625 to 0.0625
- w_up: bfloat16 [4, 7168, 2048], P('exp', None, 'ctx'), may hold values from -0.0625 to 0.0625
- w_down: bfloat16 [4, 2048, 7168], P('exp', 'ctx'), may hold values from -0.125 to 0.125
Outputs:
- attended: bfloat16 [2048, 7168], P(('ctx', 'exp'))
- expert_part: bfloat16 [2048, 7168], P(('ctx', 'exp'))
The draws below stay inside these ranges and needn't reach their ends.
Inputs may be any that keep to these rules, and one draw needn't show every extreme that they name: `routes`: each row names 8 different experts; in the rows of one device no expert in flight is named more than 8 times.
All inputs are finite; a program needn't handle non-finite values.
Results may differ from the reference program's by a relative error of at most 0.035.
Values may be sent and summed in bfloat16 or wider, within the bound.
A program may use at most 128 MiB of HBM per device.

```python
import math
import jax
import jax.numpy as jnp
from jax import lax

D = 7168
H = 64
LAT = 512
ROPE = 64
VD = 128
FF = 2048
EXPERTS = 256
TOP = 8
BLK = 128
QKW = 576
SEQ = 2048
NBLK = 16
TOK_DEV = 64
CAP = 8
FLIGHT = 4
HEADS_DEV = 16
SLICES = 8
FF_DEV = 256


def draw_latent(key, part):
    key = jax.random.fold_in(key, 3)
    field = jax.random.truncated_normal(key, -8.0, 8.0, (SEQ, QKW), jnp.float32)
    return field.astype(jnp.bfloat16)


def draw_queries(key, part):
    key = jax.random.fold_in(key, 5)
    field = jax.random.truncated_normal(key, -8.0, 8.0, (SEQ, H, QKW), jnp.float32)
    return field.reshape(SEQ, H * QKW).astype(jnp.bfloat16)


def draw_routes(key, part):
    key = jax.random.fold_in(key, 7)
    key_first, key_tail, key_rows, key_other, key_turn = jax.random.split(key, 5)
    per_owner = EXPERTS // FLIGHT
    slots = FLIGHT * CAP
    blocks = SEQ // TOK_DEV
    chosen = jax.random.randint(key_first, (blocks, 1), 0, FLIGHT).astype(jnp.int32)
    listing = (jnp.arange(slots, dtype=jnp.int32)[None, :] + chosen * CAP) % slots // CAP
    tail_perm = jax.vmap(lambda k: jax.random.permutation(k, slots - CAP))(jax.random.split(key_tail, blocks)).astype(jnp.int32)
    tail = jnp.take_along_axis(listing[:, CAP:], tail_perm, axis=1)
    listing = jnp.concatenate([listing[:, :CAP], tail], axis=1)
    if TOK_DEV > slots:
        listing = jnp.concatenate([listing, jnp.full((blocks, TOK_DEV - slots), -1, jnp.int32)], axis=1)
    row_perm = jax.vmap(lambda k: jax.random.permutation(k, TOK_DEV))(jax.random.split(key_rows, blocks)).astype(jnp.int32)
    owner_of = jnp.take_along_axis(listing, row_perm, axis=1).reshape(SEQ)
    numbers = jnp.arange(EXPERTS, dtype=jnp.int32)
    scores = jax.random.randint(key_other, (SEQ, EXPERTS), 0, 2 ** 20).astype(jnp.int32) * EXPERTS + numbers[None, :]
    scores = jnp.where((numbers % per_owner == 0)[None, :], -1, scores)
    picks = lax_top(scores)
    last = jnp.where(owner_of >= 0, owner_of * per_owner, picks[:, TOP - 1])
    lists = jnp.concatenate([picks[:, :TOP - 1], last[:, None]], axis=1)
    turn = jax.random.randint(key_turn, (SEQ, 1), 0, TOP).astype(jnp.int32)
    columns = (jnp.arange(TOP, dtype=jnp.int32)[None, :] + turn) % TOP
    return jnp.take_along_axis(lists, columns, axis=1).astype(jnp.int32)


def lax_top(scores):
    values, picks = jax.lax.top_k(scores, TOP)
    return picks.astype(jnp.int32)


def steps_of(stream_key, dims, shards, smallest, largest):
    level, own = 1.0, jax.random.fold_in(stream_key, 6)
    for position, blocks in shards:
        heights = jnp.exp(jax.random.uniform(jax.random.fold_in(own, position), (blocks,), jnp.float32, smallest / len(shards), largest / len(shards)))
        level = level * jnp.repeat(heights, dims[position] // blocks).reshape([-1 if axis == position else 1 for axis in range(len(dims))])
    return level


def bell_draw(stream_key, dims, spread, reach, shards=(), kind=jnp.bfloat16):
    array = jax.random.normal(stream_key, dims, jnp.float32) * spread
    if len(shards) > 0:
        array = steps_of(stream_key, dims, shards, -0.22, 0.18) * array
    return jnp.clip(array, min=-reach, max=reach).astype(kind)


def setup_inputs(seed: int = 0) -> dict:
    key_of = jax.random.split(jax.random.key(seed), 13)
    return {
        "queries": draw_queries(jax.random.fold_in(key_of[12], 71), 0),
        "latent": draw_latent(jax.random.fold_in(key_of[12], 71), 0),
        "block_order": jax.random.permutation(key_of[2], NBLK).astype(jnp.int32),
        "w_uv": bell_draw(key_of[3], (H, LAT, VD), LAT ** -0.5, 0.25, ((0, 4),)),
        "w_o": bell_draw(key_of[4], (H * VD, D), (H * VD) ** -0.5, 0.0625, ((0, 4), (1, 8))),
        "residual": bell_draw(key_of[5], (SEQ, D), 0.5, 4.0, ((0, 32),)),
        "norm_gain": jnp.clip(1.0 + 0.18 * jax.random.normal(key_of[6], (D,), jnp.float32), 0.099609375, 1.8984375).astype(jnp.bfloat16),
        "routes": draw_routes(jax.random.fold_in(key_of[12], 71), 0),
        "route_scores": jnp.clip(jnp.exp(math.log(1.0) - 2.9957323 * jax.random.uniform(key_of[8], (SEQ, TOP), jnp.float32) ** steps_of(key_of[8], (SEQ, TOP), ((0, 32),), -0.2, 0.2)), 0.05, 1.0),
        "w_gate": bell_draw(key_of[9], (FLIGHT, D, FF), D ** -0.5, 0.0625, ((0, 4), (2, 8))),
        "w_up": bell_draw(key_of[10], (FLIGHT, D, FF), D ** -0.5, 0.0625, ((0, 4), (2, 8))),
        "w_down": bell_draw(key_of[11], (FLIGHT, FF, D), FF ** -0.5, 0.125, ((0, 4), (1, 8))),
    }


def block_places(block_order, count):
    rows = jnp.arange(count, dtype=jnp.int32)
    return block_order[rows // BLK] * BLK + rows % BLK

def rounded(value):
    return lax.optimization_barrier(value.astype(jnp.bfloat16)).astype(jnp.float32)

def reference(queries, latent, block_order, w_uv, w_o, residual, norm_gain, routes, route_scores, w_gate, w_up, w_down):
    place = block_places(block_order, SEQ)
    allowed = place[None, :] <= place[:, None]
    values = latent[:, :LAT]
    scale = (VD + ROPE) ** (-0.5)
    per_head = jnp.swapaxes(queries.reshape(SEQ, H, QKW), 0, 1)

    def one_head(query):
        scores = jnp.dot(query, latent.T, preferred_element_type=jnp.float32) * scale
        scores = jnp.where(allowed, scores, -1e+30)
        highest = lax.optimization_barrier(jnp.max(scores, axis=1, keepdims=True))
        weights = jnp.where(allowed, jnp.exp(scores - highest), 0.0)
        total = lax.optimization_barrier(jnp.sum(weights, axis=1, keepdims=True))
        mixed = jnp.dot(weights.astype(jnp.bfloat16), values, preferred_element_type=jnp.float32)
        return (mixed / total).astype(jnp.bfloat16)
    attn_latent = lax.map(one_head, per_head)
    heads = jnp.einsum('hsl,hlv->shv', attn_latent.astype(jnp.float32), w_uv.astype(jnp.float32)).astype(jnp.bfloat16)
    heads = heads.reshape(SEQ, H * VD)
    width = HEADS_DEV * VD
    running = residual.astype(jnp.float32)
    for group in range(FLIGHT):
        term = jnp.dot(heads[:, group * width:(group + 1) * width], w_o[group * width:(group + 1) * width], preferred_element_type=jnp.float32)
        running = running + rounded(term)
    attended = running.astype(jnp.bfloat16)
    level = attended.astype(jnp.float32)
    normed = (level * lax.rsqrt(lax.optimization_barrier(jnp.mean(level * level, axis=1, keepdims=True)) + 1e-06) * norm_gain.astype(jnp.float32)).astype(jnp.bfloat16)
    share = 2.5 * route_scores / lax.optimization_barrier(jnp.sum(route_scores, axis=1, keepdims=True))
    per_owner = EXPERTS // FLIGHT
    blocks = SEQ // TOK_DEV
    slot_count = blocks * CAP
    token_ids = jnp.arange(SEQ, dtype=jnp.int32)
    combined = jnp.zeros((SEQ, D), jnp.float32)
    for owner in range(FLIGHT):
        match = routes == owner * per_owner
        hits = lax.optimization_barrier(jnp.sum(match.astype(jnp.int32), axis=1))
        weight = lax.optimization_barrier(jnp.sum(jnp.where(match, share, 0.0), axis=1))
        ranking = jnp.cumsum(hits.reshape(blocks, TOK_DEV), axis=1).reshape(SEQ) - 1
        target = jnp.where(hits > 0, token_ids // TOK_DEV * CAP + ranking, slot_count).astype(jnp.int32)
        source = jnp.full((slot_count,), SEQ, jnp.int32).at[target].set(token_ids, mode='drop')
        clipped = jnp.minimum(source, SEQ - 1).astype(jnp.int32)
        picked = normed[clipped]
        gate = jnp.dot(picked, w_gate[owner], preferred_element_type=jnp.float32)
        lifted = jnp.dot(picked, w_up[owner], preferred_element_type=jnp.float32)
        hidden = (jax.nn.silu(gate) * lifted).astype(jnp.bfloat16)
        lowered = jnp.zeros((slot_count, D), jnp.float32)
        for piece in range(SLICES):
            first = piece * FF_DEV
            lowered = lowered + rounded(jnp.dot(hidden[:, first:first + FF_DEV], w_down[owner, first:first + FF_DEV], preferred_element_type=jnp.float32))
        expert_rows = rounded(lowered)
        contribution = jnp.where((source < SEQ)[:, None], expert_rows * weight[clipped][:, None], 0.0)
        combined = combined.at[source].add(contribution, mode='drop')
    return (attended, combined.astype(jnp.bfloat16))
```

```python
import math

import jax
import jax.numpy as jnp
from jax import lax
from jax.sharding import PartitionSpec as P

EXPERTS = 256
TOP = 8
BLK = 128
PAIR = 2


def block_places(block_order, rows):
    table = jnp.arange(block_order.shape[0], dtype=jnp.int32)
    pick = (rows // BLK)[:, None] == table[None, :]
    first = jnp.sum(jnp.where(pick, block_order[None, :], 0), axis=1)
    return first * BLK + rows % BLK


def attend(carry, piece, flat_query, query_place, block_order, scale, latent_width):
    length = piece.shape[0]
    part = math.gcd(length, 512)

    def one_part(index, state):
        keys = lax.dynamic_slice_in_dim(piece, index * part, part, 0)
        offset = index * part + jnp.arange(part, dtype=jnp.int32)
        allowed = block_places(block_order, offset)[None, :] <= query_place[:, None]

        def update(inner):
            highest, total, weighted = inner
            scores = (
                lax.dot_general(
                    flat_query, keys, (((1,), (1,)), ((), ())), preferred_element_type=jnp.float32
                )
                * scale
            )
            scores = jnp.where(allowed, scores, -1e30)
            newest = jnp.maximum(highest, jnp.max(scores, axis=1))
            shrink = jnp.exp(highest - newest)
            weights = jnp.where(allowed, jnp.exp(scores - newest[:, None]), 0.0)
            total = total * shrink + jnp.sum(weights, axis=1)
            weighted = weighted * shrink[:, None] + jnp.dot(
                weights.astype(jnp.bfloat16),
                keys[:, :latent_width],
                preferred_element_type=jnp.float32,
            )
            return (newest, total, weighted)

        return lax.cond(jnp.any(allowed), update, lambda inner: inner, state)

    return lax.fori_loop(0, length // part, one_part, carry)


def per_device(
    queries,
    latent,
    block_order,
    w_uv,
    w_o,
    residual,
    norm_gain,
    routes,
    route_scores,
    w_gate,
    w_up,
    w_down,
):
    owner_count = lax.axis_size("exp")
    seq_block = queries.shape[0]
    head_count, latent_width, value_width = w_uv.shape
    key_width = latent.shape[1]
    token_count = residual.shape[0]
    model_width = residual.shape[1]
    scale = (value_width + key_width - latent_width) ** (-0.5)
    rows_here = lax.axis_index("ctx") * seq_block + jnp.arange(seq_block, dtype=jnp.int32)
    query_place = jnp.repeat(block_places(block_order, rows_here), head_count)
    flat_query = queries.reshape(seq_block * head_count, key_width)
    query_rows = seq_block * head_count
    start_state = (
        jnp.full((query_rows,), -1e30, jnp.float32),
        jnp.zeros((query_rows,), jnp.float32),
        jnp.zeros((query_rows, latent_width), jnp.float32),
    )
    highest, total, weighted = attend(
        start_state,
        lax.all_gather(latent, "ctx", axis=0, tiled=True),
        flat_query,
        query_place,
        block_order,
        scale,
        latent_width,
    )
    attn_latent = (
        (weighted / total[:, None])
        .astype(jnp.bfloat16)
        .reshape(seq_block, head_count, latent_width)
    )
    heads = jnp.einsum(
        "thl,hlv->thv", attn_latent, w_uv, preferred_element_type=jnp.float32
    ).astype(jnp.bfloat16)
    heads = heads.reshape(seq_block, head_count * value_width)
    ctx_count = lax.axis_size("ctx")
    levels = ctx_count // PAIR
    other = lax.ppermute(w_o, "ctx", [(c, c ^ 1) for c in range(ctx_count)])
    first = lax.axis_index("ctx") % PAIR == 0
    pair_columns = jnp.concatenate(
        [jnp.where(first, w_o, other), jnp.where(first, other, w_o)], axis=1
    )
    lines = [[level * PAIR + side for level in range(levels)] for side in range(PAIR)]
    line_heads = lax.all_gather(heads, "ctx", axis=0, tiled=True, axis_index_groups=lines)
    terms = jnp.dot(line_heads, pair_columns, preferred_element_type=jnp.float32).astype(
        jnp.bfloat16
    )
    width = terms.shape[1]
    terms = jnp.swapaxes(terms.reshape(levels, owner_count, token_count, width), 0, 1)
    summed = lax.psum_scatter(
        terms.reshape(owner_count * levels * token_count, width),
        "exp",
        scatter_dimension=0,
        tiled=True,
    ).reshape(levels, token_count, width)
    spread = lax.all_to_all(
        summed, "ctx", split_axis=0, concat_axis=0, tiled=True, axis_index_groups=lines
    )
    projected = (
        jnp.swapaxes(spread, 0, 1).reshape(token_count, model_width).astype(jnp.float32)
    )
    attended = (residual.astype(jnp.float32) + projected).astype(jnp.bfloat16)
    level = attended.astype(jnp.float32)
    normed = (
        level
        * lax.rsqrt(jnp.mean(level * level, axis=1, keepdims=True) + 1e-06)
        * norm_gain.astype(jnp.float32)
    ).astype(jnp.bfloat16)
    share = 2.5 * route_scores / jnp.sum(route_scores, axis=1, keepdims=True)
    per_owner = EXPERTS // owner_count
    chosen = jnp.arange(owner_count, dtype=jnp.int32) * per_owner
    match = routes[:, :, None] == chosen[None, None, :]
    hits = jnp.sum(match.astype(jnp.int32), axis=1)
    weight_to = jnp.sum(jnp.where(match, share[:, :, None], 0.0), axis=1)
    ranking = jnp.cumsum(hits, axis=0) - 1
    capacity = max(2, 4 * token_count * TOP // EXPERTS)
    slot_ids = jnp.arange(capacity, dtype=jnp.int32)
    select = ((hits[:, :, None] == 1) & (ranking[:, :, None] == slot_ids[None, None, :])).astype(
        jnp.bfloat16
    )
    outgoing = jnp.einsum("toc,td->ocd", select, normed, preferred_element_type=jnp.float32).astype(
        jnp.bfloat16
    )
    arrived = lax.all_to_all(outgoing, "exp", split_axis=0, concat_axis=0, tiled=True)
    flat_rows = arrived.reshape(owner_count * capacity, model_width)
    piece = lax.all_gather(flat_rows, "ctx", axis=0, tiled=True)
    gate = jnp.dot(piece, w_gate[0], preferred_element_type=jnp.float32)
    lifted = jnp.dot(piece, w_up[0], preferred_element_type=jnp.float32)
    hidden = (jax.nn.silu(gate) * lifted).astype(jnp.bfloat16)
    lowered = lax.psum_scatter(
        jnp.dot(hidden, w_down[0], preferred_element_type=jnp.float32).astype(jnp.bfloat16),
        "ctx",
        scatter_dimension=0,
        tiled=True,
    )
    expert_out = lowered.reshape(owner_count, capacity, model_width)
    returned = lax.all_to_all(expert_out, "exp", split_axis=0, concat_axis=0, tiled=True)
    picked = jnp.einsum("toc,ocd->otd", select, returned, preferred_element_type=jnp.float32)
    expert_part = jnp.sum(picked * jnp.transpose(weight_to)[:, :, None], axis=0).astype(
        jnp.bfloat16
    )
    return (attended, expert_part)


def solution(mesh):
    return jax.shard_map(
        per_device,
        mesh=mesh,
        in_specs=(
            P("ctx", "exp"),
            P("ctx", None),
            P(),
            P("exp", None, None),
            P("exp", "ctx"),
            P(("ctx", "exp"), None),
            P(),
            P(("ctx", "exp"), None),
            P(("ctx", "exp"), None),
            P("exp", None, "ctx"),
            P("exp", None, "ctx"),
            P("exp", "ctx", None),
        ),
        out_specs=(P(("ctx", "exp"), None), P(("ctx", "exp"), None)),
        check_vma=False,
    )
```

```python
import functools

import jax
import jax.numpy as jnp
from jax import lax
from jax.experimental import pallas as pl
from jax.experimental.pallas import tpu as pltpu
from jax.sharding import PartitionSpec as P

EXPERTS = 256
TOP = 8
BLK = 128
PAIR = 2


def block_places(block_order, rows):
    table = jnp.arange(block_order.shape[0], dtype=jnp.int32)
    pick = (rows // BLK)[:, None] == table[None, :]
    first = jnp.sum(jnp.where(pick, block_order[None, :], 0), axis=1)
    return first * BLK + rows % BLK


def attend_heads(scale, query_ref, keys_ref, flipped_ref, query_place_ref, key_place_ref, w_uv_ref, out_ref):
    width = flipped_ref.shape[0]
    latent_width, value_width = w_uv_ref.shape[1:]
    allowed = key_place_ref[...] <= query_place_ref[...]
    for head in range(w_uv_ref.shape[0]):
        query = query_ref[:, head * width : (head + 1) * width]
        scores = jnp.dot(query, flipped_ref[...], preferred_element_type=jnp.float32) * scale
        scores = jnp.where(allowed, scores, -1e30)
        highest = jnp.max(scores, axis=1, keepdims=True)
        weights = jnp.exp(scores - highest)
        total = jnp.sum(weights, axis=1, keepdims=True)
        mixed = jnp.dot(
            weights.astype(jnp.bfloat16),
            keys_ref[:, :latent_width],
            preferred_element_type=jnp.float32,
        )
        attn_latent = (mixed / total).astype(jnp.bfloat16)
        out_ref[:, head * value_width : (head + 1) * value_width] = jnp.dot(
            attn_latent, w_uv_ref[head], preferred_element_type=jnp.float32
        ).astype(jnp.bfloat16)


def attention(queries, keys, query_place, key_place, w_uv, scale):
    rows = queries.shape[0]
    head_count, latent_width, value_width = w_uv.shape
    length, width = keys.shape
    group = 2
    whole = lambda step: (0, 0)
    return pl.pallas_call(
        functools.partial(attend_heads, scale),
        grid=(head_count // group,),
        out_shape=jax.ShapeDtypeStruct((rows, head_count * value_width), jnp.bfloat16),
        in_specs=[
            pl.BlockSpec((rows, group * width), lambda step: (0, step)),
            pl.BlockSpec((length, width), whole),
            pl.BlockSpec((width, length), whole),
            pl.BlockSpec((rows, 1), whole),
            pl.BlockSpec((1, length), whole),
            pl.BlockSpec((group, latent_width, value_width), lambda step: (step, 0, 0)),
        ],
        out_specs=pl.BlockSpec((rows, group * value_width), lambda step: (0, step)),
        compiler_params=pltpu.CompilerParams(vmem_limit_bytes=52 * 2**20),
        cost_estimate=pl.CostEstimate(
            flops=2 * rows * length * head_count * (width + latent_width),
            bytes_accessed=2 * rows * head_count * (width + value_width),
            transcendentals=rows * length * head_count,
        ),
    )(queries, keys, keys.T, query_place[:, None], key_place[None, :], w_uv)


def per_device(
    queries,
    latent,
    block_order,
    w_uv,
    w_o,
    residual,
    norm_gain,
    routes,
    route_scores,
    w_gate,
    w_up,
    w_down,
):
    owner_count = lax.axis_size("exp")
    seq_block = queries.shape[0]
    head_count, latent_width, value_width = w_uv.shape
    key_width = latent.shape[1]
    token_count = residual.shape[0]
    model_width = residual.shape[1]
    scale = (value_width + key_width - latent_width) ** (-0.5)
    rows_here = lax.axis_index("ctx") * seq_block + jnp.arange(seq_block, dtype=jnp.int32)
    query_place = block_places(block_order, rows_here)
    keys = lax.all_gather(latent, "ctx", axis=0, tiled=True)
    key_place = block_places(block_order, jnp.arange(keys.shape[0], dtype=jnp.int32))
    heads = attention(queries, keys, query_place, key_place, w_uv, scale)
    ctx_count = lax.axis_size("ctx")
    levels = ctx_count // PAIR
    pairs = [[level * PAIR + side for side in range(PAIR)] for level in range(levels)]
    pair_columns = lax.all_gather(w_o, "ctx", axis=1, tiled=True, axis_index_groups=pairs)
    lines = [[level * PAIR + side for level in range(levels)] for side in range(PAIR)]
    line_heads = lax.all_gather(heads, "ctx", axis=0, tiled=True, axis_index_groups=lines)
    terms = jnp.dot(line_heads, pair_columns, preferred_element_type=jnp.float32).astype(
        jnp.bfloat16
    )
    width = terms.shape[1]
    terms = jnp.swapaxes(terms.reshape(levels, owner_count, token_count, width), 0, 1)
    summed = lax.psum_scatter(
        terms.reshape(owner_count * levels * token_count, width),
        "exp",
        scatter_dimension=0,
        tiled=True,
    ).reshape(levels, token_count, width)
    spread = lax.all_to_all(
        summed, "ctx", split_axis=0, concat_axis=0, tiled=True, axis_index_groups=lines
    )
    projected = (
        jnp.swapaxes(spread, 0, 1).reshape(token_count, model_width).astype(jnp.float32)
    )
    attended = (residual.astype(jnp.float32) + projected).astype(jnp.bfloat16)
    level = attended.astype(jnp.float32)
    normed = (
        level
        * lax.rsqrt(jnp.mean(level * level, axis=1, keepdims=True) + 1e-06)
        * norm_gain.astype(jnp.float32)
    ).astype(jnp.bfloat16)
    share = 2.5 * route_scores / jnp.sum(route_scores, axis=1, keepdims=True)
    per_owner = EXPERTS // owner_count
    chosen = jnp.arange(owner_count, dtype=jnp.int32) * per_owner
    match = routes[:, :, None] == chosen[None, None, :]
    hits = jnp.sum(match.astype(jnp.int32), axis=1)
    weight_to = jnp.sum(jnp.where(match, share[:, :, None], 0.0), axis=1)
    ranking = jnp.cumsum(hits, axis=0) - 1
    capacity = max(2, 4 * token_count * TOP // EXPERTS)
    slot_ids = jnp.arange(capacity, dtype=jnp.int32)
    select = ((hits[:, :, None] == 1) & (ranking[:, :, None] == slot_ids[None, None, :])).astype(
        jnp.bfloat16
    )
    outgoing = jnp.einsum("toc,td->ocd", select, normed, preferred_element_type=jnp.float32).astype(
        jnp.bfloat16
    )
    arrived = lax.all_to_all(outgoing, "exp", split_axis=0, concat_axis=0, tiled=True)
    flat_rows = arrived.reshape(owner_count * capacity, model_width)
    piece = lax.all_gather(flat_rows, "ctx", axis=0, tiled=True)
    gate = jnp.dot(piece, w_gate[0], preferred_element_type=jnp.float32)
    lifted = jnp.dot(piece, w_up[0], preferred_element_type=jnp.float32)
    hidden = (jax.nn.silu(gate) * lifted).astype(jnp.bfloat16)
    lowered = lax.psum_scatter(
        jnp.dot(hidden, w_down[0], preferred_element_type=jnp.float32).astype(jnp.bfloat16),
        "ctx",
        scatter_dimension=0,
        tiled=True,
    )
    expert_out = lowered.reshape(owner_count, capacity, model_width)
    returned = lax.all_to_all(expert_out, "exp", split_axis=0, concat_axis=0, tiled=True)
    picked = jnp.einsum("toc,ocd->otd", select, returned, preferred_element_type=jnp.float32)
    expert_part = jnp.sum(picked * jnp.transpose(weight_to)[:, :, None], axis=0).astype(
        jnp.bfloat16
    )
    return (attended, expert_part)


def solution(mesh):
    return jax.shard_map(
        per_device,
        mesh=mesh,
        in_specs=(
            P("ctx", "exp"),
            P("ctx", None),
            P(),
            P("exp", None, None),
            P("exp", "ctx"),
            P(("ctx", "exp"), None),
            P(),
            P(("ctx", "exp"), None),
            P(("ctx", "exp"), None),
            P("exp", None, "ctx"),
            P("exp", None, "ctx"),
            P("exp", "ctx", None),
        ),
        out_specs=(P(("ctx", "exp"), None), P(("ctx", "exp"), None)),
        check_vma=False,
    )
```

```python
import functools

import jax
import jax.numpy as jnp
from jax import lax
from jax.experimental import pallas as pl
from jax.experimental.pallas import tpu as pltpu
from jax.sharding import PartitionSpec as P

EXPERTS = 256
TOP = 8
BLK = 128
PAIR = 2
HALVES = 2


def block_places(block_order, rows):
    table = jnp.arange(block_order.shape[0], dtype=jnp.int32)
    pick = (rows // BLK)[:, None] == table[None, :]
    first = jnp.sum(jnp.where(pick, block_order[None, :], 0), axis=1)
    return first * BLK + rows % BLK


def attend_heads(scale, query_ref, keys_ref, flipped_ref, query_place_ref, key_place_ref, w_uv_ref, out_ref):
    width = flipped_ref.shape[0]
    latent_width, value_width = w_uv_ref.shape[1:]
    allowed = key_place_ref[...] <= query_place_ref[...]
    for head in range(w_uv_ref.shape[0]):
        query = query_ref[:, head * width : (head + 1) * width]
        scores = jnp.dot(query, flipped_ref[...], preferred_element_type=jnp.float32) * scale
        scores = jnp.where(allowed, scores, -1e30)
        highest = jnp.max(scores, axis=1, keepdims=True)
        weights = jnp.exp(scores - highest)
        total = jnp.sum(weights, axis=1, keepdims=True)
        mixed = jnp.dot(
            weights.astype(jnp.bfloat16),
            keys_ref[:, :latent_width],
            preferred_element_type=jnp.float32,
        )
        attn_latent = (mixed / total).astype(jnp.bfloat16)
        out_ref[:, head * value_width : (head + 1) * value_width] = jnp.dot(
            attn_latent, w_uv_ref[head], preferred_element_type=jnp.float32
        ).astype(jnp.bfloat16)


def attention(queries, keys, query_place, key_place, w_uv, scale, part, parts):
    rows = queries.shape[0]
    head_count, latent_width, value_width = w_uv.shape
    length, width = keys.shape
    group = 2
    head_count = head_count // parts
    first = part * (head_count // group)
    whole = lambda step: (0, 0)
    return pl.pallas_call(
        functools.partial(attend_heads, scale),
        grid=(head_count // group,),
        out_shape=jax.ShapeDtypeStruct((rows, head_count * value_width), jnp.bfloat16),
        in_specs=[
            pl.BlockSpec((rows, group * width), lambda step: (0, first + step)),
            pl.BlockSpec((length, width), whole),
            pl.BlockSpec((width, length), whole),
            pl.BlockSpec((rows, 1), whole),
            pl.BlockSpec((1, length), whole),
            pl.BlockSpec((group, latent_width, value_width), lambda step: (first + step, 0, 0)),
        ],
        out_specs=pl.BlockSpec((rows, group * value_width), lambda step: (0, step)),
        compiler_params=pltpu.CompilerParams(vmem_limit_bytes=52 * 2**20),
        cost_estimate=pl.CostEstimate(
            flops=2 * rows * length * head_count * (width + latent_width),
            bytes_accessed=2 * rows * head_count * (width + value_width),
            transcendentals=rows * length * head_count,
        ),
    )(queries, keys, keys.T, query_place[:, None], key_place[None, :], w_uv)


def per_device(
    queries,
    latent,
    block_order,
    w_uv,
    w_o,
    residual,
    norm_gain,
    routes,
    route_scores,
    w_gate,
    w_up,
    w_down,
):
    owner_count = lax.axis_size("exp")
    seq_block = queries.shape[0]
    head_count, latent_width, value_width = w_uv.shape
    key_width = latent.shape[1]
    token_count = residual.shape[0]
    model_width = residual.shape[1]
    scale = (value_width + key_width - latent_width) ** (-0.5)
    rows_here = lax.axis_index("ctx") * seq_block + jnp.arange(seq_block, dtype=jnp.int32)
    query_place = block_places(block_order, rows_here)
    keys = lax.all_gather(latent, "ctx", axis=0, tiled=True)
    key_place = block_places(block_order, jnp.arange(keys.shape[0], dtype=jnp.int32))
    ctx_count = lax.axis_size("ctx")
    levels = ctx_count // PAIR
    lines = [[level * PAIR + side for level in range(levels)] for side in range(PAIR)]
    other = lax.ppermute(w_o, "ctx", [(c, c ^ 1) for c in range(ctx_count)])
    depth = w_o.shape[0] // HALVES
    own_terms, other_terms = 0.0, 0.0
    for part in range(HALVES):
        heads = attention(queries, keys, query_place, key_place, w_uv, scale, part, HALVES)
        heads = lax.all_gather(heads, "ctx", axis=0, tiled=True, axis_index_groups=lines)
        rows = slice(part * depth, (part + 1) * depth)
        own_terms += jnp.dot(heads, w_o[rows], preferred_element_type=jnp.float32)
        other_terms += jnp.dot(heads, other[rows], preferred_element_type=jnp.float32)
    terms = jnp.concatenate([own_terms, other_terms], axis=1).astype(jnp.bfloat16)
    width = terms.shape[1]
    terms = jnp.swapaxes(terms.reshape(levels, owner_count, token_count, width), 0, 1)
    summed = lax.psum_scatter(
        terms.reshape(owner_count * levels * token_count, width),
        "exp",
        scatter_dimension=0,
        tiled=True,
    ).reshape(levels, token_count, width)
    spread = lax.all_to_all(
        summed, "ctx", split_axis=0, concat_axis=0, tiled=True, axis_index_groups=lines
    )
    spread = jnp.swapaxes(spread, 0, 1).reshape(token_count, levels, PAIR, width // PAIR)
    spread = jnp.where(lax.axis_index("ctx") % PAIR == 0, spread, spread[:, :, ::-1])
    projected = spread.reshape(token_count, model_width).astype(jnp.float32)
    attended = (residual.astype(jnp.float32) + projected).astype(jnp.bfloat16)
    level = attended.astype(jnp.float32)
    normed = (
        level
        * lax.rsqrt(jnp.mean(level * level, axis=1, keepdims=True) + 1e-06)
        * norm_gain.astype(jnp.float32)
    ).astype(jnp.bfloat16)
    share = 2.5 * route_scores / jnp.sum(route_scores, axis=1, keepdims=True)
    per_owner = EXPERTS // owner_count
    chosen = jnp.arange(owner_count, dtype=jnp.int32) * per_owner
    match = routes[:, :, None] == chosen[None, None, :]
    hits = jnp.sum(match.astype(jnp.int32), axis=1)
    weight_to = jnp.sum(jnp.where(match, share[:, :, None], 0.0), axis=1)
    ranking = jnp.cumsum(hits, axis=0) - 1
    capacity = max(2, 4 * token_count * TOP // EXPERTS)
    slot_ids = jnp.arange(capacity, dtype=jnp.int32)
    select = ((hits[:, :, None] == 1) & (ranking[:, :, None] == slot_ids[None, None, :])).astype(
        jnp.bfloat16
    )
    outgoing = jnp.einsum("toc,td->ocd", select, normed, preferred_element_type=jnp.float32).astype(
        jnp.bfloat16
    )
    arrived = lax.all_to_all(outgoing, "exp", split_axis=0, concat_axis=0, tiled=True)
    flat_rows = arrived.reshape(owner_count * capacity, model_width)
    piece = lax.all_gather(flat_rows, "ctx", axis=0, tiled=True)
    gate = jnp.dot(piece, w_gate[0], preferred_element_type=jnp.float32)
    lifted = jnp.dot(piece, w_up[0], preferred_element_type=jnp.float32)
    hidden = (jax.nn.silu(gate) * lifted).astype(jnp.bfloat16)
    lowered = lax.psum_scatter(
        jnp.dot(hidden, w_down[0], preferred_element_type=jnp.float32).astype(jnp.bfloat16),
        "ctx",
        scatter_dimension=0,
        tiled=True,
    )
    expert_out = lowered.reshape(owner_count, capacity, model_width)
    returned = lax.all_to_all(expert_out, "exp", split_axis=0, concat_axis=0, tiled=True)
    picked = jnp.einsum("toc,ocd->otd", select, returned, preferred_element_type=jnp.float32)
    expert_part = jnp.sum(picked * jnp.transpose(weight_to)[:, :, None], axis=0).astype(
        jnp.bfloat16
    )
    return (attended, expert_part)


def solution(mesh):
    return jax.shard_map(
        per_device,
        mesh=mesh,
        in_specs=(
            P("ctx", "exp"),
            P("ctx", None),
            P(),
            P("exp", None, None),
            P("exp", "ctx"),
            P(("ctx", "exp"), None),
            P(),
            P(("ctx", "exp"), None),
            P(("ctx", "exp"), None),
            P("exp", None, "ctx"),
            P("exp", None, "ctx"),
            P("exp", "ctx", None),
        ),
        out_specs=(P(("ctx", "exp"), None), P(("ctx", "exp"), None)),
        check_vma=False,
    )
```

```python
import functools

import jax
import jax.numpy as jnp
from jax import lax
from jax.experimental import pallas as pl
from jax.experimental.pallas import tpu as pltpu
from jax.sharding import PartitionSpec as P

EXPERTS = 256
TOP = 8
BLK = 128
PAIR = 2
HALVES = 2


def block_places(block_order, rows):
    table = jnp.arange(block_order.shape[0], dtype=jnp.int32)
    pick = (rows // BLK)[:, None] == table[None, :]
    first = jnp.sum(jnp.where(pick, block_order[None, :], 0), axis=1)
    return first * BLK + rows % BLK


def attend_heads(scale, query_ref, keys_ref, flipped_ref, query_place_ref, key_place_ref, w_uv_ref, out_ref):
    width = flipped_ref.shape[0]
    latent_width, value_width = w_uv_ref.shape[1:]
    allowed = key_place_ref[...] <= query_place_ref[...]
    for head in range(w_uv_ref.shape[0]):
        query = query_ref[:, head * width : (head + 1) * width]
        scores = jnp.dot(query, flipped_ref[...], preferred_element_type=jnp.float32) * scale
        scores = jnp.where(allowed, scores, -1e30)
        highest = jnp.max(scores, axis=1, keepdims=True)
        weights = jnp.exp(scores - highest)
        total = jnp.sum(weights, axis=1, keepdims=True)
        mixed = jnp.dot(
            weights.astype(jnp.bfloat16),
            keys_ref[:, :latent_width],
            preferred_element_type=jnp.float32,
        )
        attn_latent = (mixed / total).astype(jnp.bfloat16)
        out_ref[:, head * value_width : (head + 1) * value_width] = jnp.dot(
            attn_latent, w_uv_ref[head], preferred_element_type=jnp.float32
        ).astype(jnp.bfloat16)


def attention(queries, keys, query_place, key_place, w_uv, scale, part, parts):
    rows = queries.shape[0]
    head_count, latent_width, value_width = w_uv.shape
    length, width = keys.shape
    group = 2
    head_count = head_count // parts
    first = part * (head_count // group)
    whole = lambda step: (0, 0)
    return pl.pallas_call(
        functools.partial(attend_heads, scale),
        grid=(head_count // group,),
        out_shape=jax.ShapeDtypeStruct((rows, head_count * value_width), jnp.bfloat16),
        in_specs=[
            pl.BlockSpec((rows, group * width), lambda step: (0, first + step)),
            pl.BlockSpec((length, width), whole),
            pl.BlockSpec((width, length), whole),
            pl.BlockSpec((rows, 1), whole),
            pl.BlockSpec((1, length), whole),
            pl.BlockSpec((group, latent_width, value_width), lambda step: (first + step, 0, 0)),
        ],
        out_specs=pl.BlockSpec((rows, group * value_width), lambda step: (0, step)),
        compiler_params=pltpu.CompilerParams(vmem_limit_bytes=52 * 2**20),
        cost_estimate=pl.CostEstimate(
            flops=2 * rows * length * head_count * (width + latent_width),
            bytes_accessed=2 * rows * head_count * (width + value_width),
            transcendentals=rows * length * head_count,
        ),
    )(queries, keys, keys.T, query_place[:, None], key_place[None, :], w_uv)


def per_device(
    queries,
    latent,
    block_order,
    w_uv,
    w_o,
    residual,
    norm_gain,
    routes,
    route_scores,
    w_gate,
    w_up,
    w_down,
):
    owner_count = lax.axis_size("exp")
    seq_block = queries.shape[0]
    head_count, latent_width, value_width = w_uv.shape
    key_width = latent.shape[1]
    token_count = residual.shape[0]
    model_width = residual.shape[1]
    scale = (value_width + key_width - latent_width) ** (-0.5)
    rows_here = lax.axis_index("ctx") * seq_block + jnp.arange(seq_block, dtype=jnp.int32)
    query_place = block_places(block_order, rows_here)
    keys = lax.all_gather(latent, "ctx", axis=0, tiled=True)
    key_place = block_places(block_order, jnp.arange(keys.shape[0], dtype=jnp.int32))
    ctx_count = lax.axis_size("ctx")
    levels = ctx_count // PAIR
    lines = [[level * PAIR + side for level in range(levels)] for side in range(PAIR)]
    swap = [(c, c ^ 1) for c in range(ctx_count)]
    other = lax.ppermute(w_o, "ctx", swap)
    depth = w_o.shape[0] // HALVES
    terms = [0.0, 0.0]
    for part in range(HALVES):
        heads = attention(queries, keys, query_place, key_place, w_uv, scale, part, HALVES)
        heads = lax.all_gather(heads, "ctx", axis=0, tiled=True, axis_index_groups=lines)
        rows = slice(part * depth, (part + 1) * depth)
        for side, columns in enumerate((w_o, other)):
            terms[side] += jnp.dot(heads, columns[rows], preferred_element_type=jnp.float32)
    spread = []
    for term in terms:
        width = term.shape[1]
        term = term.astype(jnp.bfloat16).reshape(levels, owner_count, token_count, width)
        summed = lax.psum_scatter(
            jnp.swapaxes(term, 0, 1).reshape(owner_count * levels * token_count, width),
            "exp",
            scatter_dimension=0,
            tiled=True,
        ).reshape(levels, token_count, width)
        spread.append(
            lax.all_to_all(
                summed, "ctx", split_axis=0, concat_axis=0, tiled=True, axis_index_groups=lines
            )
        )
    is_first = lax.axis_index("ctx") % PAIR == 0
    projected = jnp.stack(
        [jnp.where(is_first, *spread), jnp.where(is_first, *spread[::-1])], axis=1
    )
    projected = (
        jnp.transpose(projected, (2, 0, 1, 3))
        .reshape(token_count, model_width)
        .astype(jnp.float32)
    )
    attended = (residual.astype(jnp.float32) + projected).astype(jnp.bfloat16)
    level = attended.astype(jnp.float32)
    normed = (
        level
        * lax.rsqrt(jnp.mean(level * level, axis=1, keepdims=True) + 1e-06)
        * norm_gain.astype(jnp.float32)
    ).astype(jnp.bfloat16)
    share = 2.5 * route_scores / jnp.sum(route_scores, axis=1, keepdims=True)
    per_owner = EXPERTS // owner_count
    chosen = jnp.arange(owner_count, dtype=jnp.int32) * per_owner
    match = routes[:, :, None] == chosen[None, None, :]
    hits = jnp.sum(match.astype(jnp.int32), axis=1)
    weight_to = jnp.sum(jnp.where(match, share[:, :, None], 0.0), axis=1)
    ranking = jnp.cumsum(hits, axis=0) - 1
    capacity = max(2, 4 * token_count * TOP // EXPERTS)
    slot_ids = jnp.arange(capacity, dtype=jnp.int32)
    select = ((hits[:, :, None] == 1) & (ranking[:, :, None] == slot_ids[None, None, :])).astype(
        jnp.bfloat16
    )
    outgoing = jnp.einsum("toc,td->ocd", select, normed, preferred_element_type=jnp.float32).astype(
        jnp.bfloat16
    )
    arrived = lax.all_to_all(outgoing, "exp", split_axis=0, concat_axis=0, tiled=True)
    flat_rows = arrived.reshape(owner_count * capacity, model_width)
    piece = lax.all_gather(flat_rows, "ctx", axis=0, tiled=True)
    gate = jnp.dot(piece, w_gate[0], preferred_element_type=jnp.float32)
    lifted = jnp.dot(piece, w_up[0], preferred_element_type=jnp.float32)
    hidden = (jax.nn.silu(gate) * lifted).astype(jnp.bfloat16)
    slots = owner_count * capacity
    hidden = hidden.reshape(levels, PAIR, slots, hidden.shape[1])
    for_own = jnp.where(is_first, hidden[:, 0], hidden[:, 1]).reshape(levels * slots, -1)
    for_other = jnp.where(is_first, hidden[:, 1], hidden[:, 0]).reshape(levels * slots, -1)
    lowered = []
    for part in range(HALVES):
        span = model_width // HALVES
        down = w_down[0][:, part * span : (part + 1) * span]
        sent = lax.ppermute(
            jnp.dot(for_other, down, preferred_element_type=jnp.float32).astype(jnp.bfloat16),
            "ctx",
            swap,
        )
        kept = jnp.dot(for_own, down, preferred_element_type=jnp.float32)
        lowered.append(
            lax.psum_scatter(
                (kept + sent.astype(jnp.float32)).astype(jnp.bfloat16),
                "ctx",
                scatter_dimension=0,
                tiled=True,
                axis_index_groups=lines,
            )
        )
    lowered = jnp.concatenate(lowered, axis=1)
    expert_out = lowered.reshape(owner_count, capacity, model_width)
    returned = lax.all_to_all(expert_out, "exp", split_axis=0, concat_axis=0, tiled=True)
    picked = jnp.einsum("toc,ocd->otd", select, returned, preferred_element_type=jnp.float32)
    expert_part = jnp.sum(picked * jnp.transpose(weight_to)[:, :, None], axis=0).astype(
        jnp.bfloat16
    )
    return (attended, expert_part)


def solution(mesh):
    return jax.shard_map(
        per_device,
        mesh=mesh,
        in_specs=(
            P("ctx", "exp"),
            P("ctx", None),
            P(),
            P("exp", None, None),
            P("exp", "ctx"),
            P(("ctx", "exp"), None),
            P(),
            P(("ctx", "exp"), None),
            P(("ctx", "exp"), None),
            P("exp", None, "ctx"),
            P("exp", None, "ctx"),
            P("exp", "ctx", None),
        ),
        out_specs=(P(("ctx", "exp"), None), P(("ctx", "exp"), None)),
        check_vma=False,
    )
```
